32 devices in a mesh: au: 4 (over y, x), ia: 8 (over z, core).
Axes of the slice: x: 2, y: 2, z: 4, core: 2. Of those that a mesh axis runs over, the one named last changes fastest.
Arguments:
- user_emb: bfloat16 [4096, 128], P(('au', 'ia')), may hold values from -1.75 to 1.75
- item_emb: bfloat16 [16384, 128], P(('au', 'ia')), may hold values from -1.75 to 1.75
- user_cot: bfloat16 [4096, 128], P(('au', 'ia')), may hold values from -6 to 6
- item_cot: bfloat16 [16384, 128], P(('au', 'ia')), may hold values from -6 to 6
- user_degree: int32 [4096], P('au'), may hold values from 8 to 31
- item_degree: int32 [4, 8, 512], P(None, 'ia'), may hold values from 2 to 7
- tile_rows: int32 [4, 8, 24], P('au', 'ia'), may hold values from 0 to 3, as said below
- tile_cols: int32 [4, 8, 24], P('au', 'ia'), may hold values from 0 to 7
- tile_key: int32 [4, 8, 24], P('au', 'ia'), may hold values from 0 to 4095
- tile_count: int32 [4, 8], P('au', 'ia'), may hold values from 1 to 24, as said below
Outputs:
- user_final: bfloat16 [4096, 128], P(('au', 'ia'))
- item_final: bfloat16 [16384, 128], P(('au', 'ia'))
- user_grad: float32 [4096, 128], P(('au', 'ia'))
- item_grad: float32 [16384, 128], P(('au', 'ia'))
The draws below stay inside these ranges and needn't reach their ends.
Inputs may be any that keep to these rules, and one draw needn't show every extreme that they name: On each device the first tile_count entries of tile_rows and tile_cols name distinct tiles; later entries are not read. `tile_count`: some device has exactly 24 occupied tiles in every draw.
All inputs are finite; a program needn't handle non-finite values.
Results may differ from the reference program's by a relative error of at most 0.012.
Values may be sent and summed in bfloat16 or wider, within the bound.
A program may use at most 64 MiB of HBM per device.

```python
import jax
import jax.numpy as jnp
from jax import lax

EMB = 128
TILE = 256
U_TILES = 4
I_TILES = 8
TMAX = 24
U_BLOCK = 1024
I_BLOCK = 2048
I_SHARD = 512
USERS = 4096
ITEMS = 16384
EDGES_U = 256
N_AU = 4
N_IA = 8


def occupied_slots(key):
    key_list = jax.random.split(key, N_AU * N_IA)
    orders = jax.vmap(lambda one_key: jax.random.permutation(one_key, U_TILES * I_TILES))(key_list)
    return orders[:, :TMAX].reshape(N_AU, N_IA, TMAX).astype(jnp.int32)


def draw_tile_rows(key, part):
    return occupied_slots(key) // I_TILES


def draw_tile_cols(key, part):
    return occupied_slots(key) % I_TILES


def draw_tile_count(key, part):
    key = jax.random.fold_in(key, 3)
    first_key, second_key = jax.random.split(key)
    spread = jax.random.randint(first_key, (N_AU * N_IA,), 0, TMAX)
    counts = 1 + spread * spread // (TMAX - 1)
    fullest = jax.random.randint(second_key, (), 0, N_AU * N_IA)
    counts = counts.at[fullest].set(TMAX)
    return counts.reshape(N_AU, N_IA).astype(jnp.int32)


def touch_ends(result, rng, low, high):
    index_at = [jax.random.randint(jax.random.fold_in(rng, axis), (), 0, length) for axis, length in enumerate(result.shape)]
    main_axis = result.shape.index(max(result.shape))
    neighbour = index_at[:main_axis] + [(index_at[main_axis] + 1) % result.shape[main_axis]] + index_at[main_axis + 1:]
    return result.at[tuple(index_at)].set(low).at[tuple(neighbour)].set(high)


def shard_levels(stream_key, dims, shards, least, high):
    level, own = 1.0, jax.random.fold_in(stream_key, 6)
    for position, shards_of in shards:
        draws = jnp.exp(jax.random.uniform(jax.random.fold_in(own, position), (shards_of,), jnp.float32, least / len(shards), high / len(shards)))
        level = level * jnp.repeat(draws, dims[position] // shards_of).reshape([-1 if axis == position else 1 for axis in range(len(dims))])
    return level


def noise(stream_key, shape, deviation, limit, shards=(), kind=jnp.bfloat16):
    entries = deviation * jax.random.normal(stream_key, shape, jnp.float32)
    if shards:
        entries = entries * shard_levels(stream_key, shape, shards, -0.22, 0.18)
    return jnp.clip(entries, -limit, limit).astype(kind)


def setup_inputs(seed: int = 0) -> dict:
    streams_of = jax.random.split(jax.random.key(seed), 11)
    return {
        "user_emb": noise(streams_of[0], (USERS, EMB), 0.3, 1.75, ((0, 32),)),
        "item_emb": noise(streams_of[1], (ITEMS, EMB), 0.3, 1.75, ((0, 32),)),
        "user_cot": noise(streams_of[2], (USERS, EMB), 1.0, 6.0, ((0, 32),)),
        "item_cot": noise(streams_of[3], (ITEMS, EMB), 1.0, 6.0, ((0, 32),)),
        "user_degree": touch_ends(jax.random.randint(streams_of[4], (USERS,), EDGES_U // 32, EDGES_U // 8), jax.random.fold_in(streams_of[4], 1), EDGES_U // 32, (EDGES_U // 8) - 1).astype(jnp.int32),
        "item_degree": touch_ends(jax.random.randint(streams_of[5], (N_AU, N_IA, I_SHARD), 2, 8), jax.random.fold_in(streams_of[5], 1), 2, 7).astype(jnp.int32),
        "tile_rows": draw_tile_rows(jax.random.fold_in(streams_of[10], 71), 0),
        "tile_cols": draw_tile_cols(jax.random.fold_in(streams_of[10], 71), 0),
        "tile_key": touch_ends(jax.random.randint(streams_of[8], (N_AU, N_IA, TMAX), 0, 4096), jax.random.fold_in(streams_of[8], 1), 0, 4095).astype(jnp.int32),
        "tile_count": draw_tile_count(jax.random.fold_in(streams_of[10], 71), 0),
    }


def edge_mask(size, tile_number):
    row_ids = lax.broadcasted_iota(jnp.int32, (size, size), 0)
    col_ids = lax.broadcasted_iota(jnp.int32, (size, size), 1)
    hashed = (row_ids * 977 + tile_number * 263) % 8191
    hashed = (hashed * hashed % 8191 + col_ids * 1531) % 8191
    hashed = hashed * hashed % 8191
    return jnp.where(hashed % 8 == 0, 1.0, 0.0).astype(jnp.float32)

def gate_weight(user_rows, item_rows, user_norm, item_norm, tile_number):
    logits = lax.dot_general(user_rows, item_rows, (((1,), (1,)), ((), ())), preferred_element_type=jnp.float32)
    gate_value = jax.nn.sigmoid(logits)
    weight = edge_mask(user_rows.shape[0], tile_number) / jnp.sqrt(user_norm[:, None] * item_norm[None, :])
    return (gate_value, weight)

def left_product(matrix, other):
    return lax.dot_general(matrix, other, (((0,), (0,)), ((), ())), preferred_element_type=jnp.float32)

def right_product(matrix, other):
    return lax.dot_general(matrix, other, (((1,), (1,)), ((), ())), preferred_element_type=jnp.float32)

def add_block(running, offset, addend):
    current = lax.dynamic_slice_in_dim(running, offset, addend.shape[0], 0)
    return lax.dynamic_update_slice_in_dim(running, current + addend, offset, 0)

def to_item_order(blocked):
    width_now = blocked.shape[-1]
    return blocked.reshape(N_IA, N_AU, I_SHARD, width_now).transpose(1, 0, 2, 3).reshape(ITEMS, width_now)

def to_column_blocks(items):
    width_now = items.shape[-1]
    return items.reshape(N_AU, N_IA, I_SHARD, width_now).transpose(1, 0, 2, 3).reshape(N_IA, I_BLOCK, width_now)

def rounded_sum(partial_sum):
    return lax.optimization_barrier(partial_sum.astype(jnp.bfloat16)).astype(jnp.float32)

def run_section(first_users, first_items, later_users, later_items, user_degree, item_degree, tile_rows, tile_cols, tile_key, tile_count):
    row_table = tile_rows.reshape(N_AU * N_IA, TMAX)
    col_table = tile_cols.reshape(N_AU * N_IA, TMAX)
    key_table = tile_key.reshape(N_AU * N_IA, TMAX)
    count_table = tile_count.reshape(N_AU * N_IA)

    def one_device(carry, device):
        user_acc, item_acc = carry
        row_block = device // N_IA
        col_block = device % N_IA
        block_start = row_block * U_BLOCK
        block_users = lax.dynamic_slice_in_dim(first_users, block_start, U_BLOCK, 0)
        block_items = lax.dynamic_index_in_dim(first_items, col_block, 0, keepdims=False)
        user_norm = lax.dynamic_slice_in_dim(user_degree, block_start, U_BLOCK, 0).astype(jnp.float32)
        item_norm = lax.dynamic_index_in_dim(item_degree, col_block, 1, keepdims=False).reshape(I_BLOCK).astype(jnp.float32)
        row_ids = lax.dynamic_index_in_dim(row_table, device, 0, keepdims=False)
        col_ids = lax.dynamic_index_in_dim(col_table, device, 0, keepdims=False)
        key_ids = lax.dynamic_index_in_dim(key_table, device, 0, keepdims=False)
        if later_users is not None:
            block_later_users = lax.dynamic_slice_in_dim(later_users, block_start, U_BLOCK, 0)
            block_later_items = lax.dynamic_index_in_dim(later_items, col_block, 0, keepdims=False)

        def step(slot_index, partials):
            user_start = row_ids[slot_index] * TILE
            item_start = col_ids[slot_index] * TILE
            first_user = lax.dynamic_slice_in_dim(block_users, user_start, TILE, 0)
            first_item = lax.dynamic_slice_in_dim(block_items, item_start, TILE, 0)
            gate_value, weight = gate_weight(first_user[:, :EMB], first_item[:, :EMB], lax.dynamic_slice_in_dim(user_norm, user_start, TILE, 0), lax.dynamic_slice_in_dim(item_norm, item_start, TILE, 0), key_ids[slot_index])
            adjacency = (gate_value * weight).astype(jnp.bfloat16)
            if later_users is None:
                user_term = jnp.dot(adjacency, first_item, preferred_element_type=jnp.float32)
                item_term = left_product(adjacency, first_user)
            else:
                later_user = lax.dynamic_slice_in_dim(block_later_users, user_start, TILE, 0)
                later_item = lax.dynamic_slice_in_dim(block_later_items, item_start, TILE, 0)
                slope = right_product(first_user[:, :EMB], later_item[:, EMB:])
                slope = slope + right_product(first_user[:, EMB:], later_item[:, :EMB])
                slope = slope + right_product(later_user[:, :EMB], first_item[:, EMB:])
                slope = slope + right_product(later_user[:, EMB:], first_item[:, :EMB])
                descent = (slope * weight * gate_value * (1.0 - gate_value)).astype(jnp.bfloat16)
                product = jnp.dot(adjacency, later_item, preferred_element_type=jnp.float32)
                user_term = jnp.concatenate([product[:, :EMB], product[:, EMB:] + jnp.dot(descent, first_item[:, :EMB], preferred_element_type=jnp.float32)], axis=1)
                product = left_product(adjacency, later_user)
                item_term = jnp.concatenate([product[:, :EMB], product[:, EMB:] + left_product(descent, first_user[:, :EMB])], axis=1)
            return (add_block(partials[0], user_start, user_term), add_block(partials[1], item_start, item_term))
        zero_users = jnp.zeros((U_BLOCK, 2 * EMB), jnp.float32)
        zero_items = jnp.zeros((I_BLOCK, 2 * EMB), jnp.float32)
        user_part, item_part = lax.fori_loop(0, count_table[device], step, (zero_users, zero_items))
        user_acc = add_block(user_acc, block_start, rounded_sum(user_part))
        item_acc = item_acc.at[col_block].add(rounded_sum(item_part))
        return ((user_acc, item_acc), None)
    start_carry = (jnp.zeros((USERS, 2 * EMB), jnp.float32), jnp.zeros((N_IA, I_BLOCK, 2 * EMB), jnp.float32))
    finished, unused = lax.scan(one_device, start_carry, jnp.arange(N_AU * N_IA, dtype=jnp.int32))
    return finished

def reference(user_emb, item_emb, user_cot, item_cot, user_degree, item_degree, tile_rows, tile_cols, tile_key, tile_count):
    first_users = jnp.concatenate([user_emb, user_cot], axis=1)
    first_items = to_column_blocks(jnp.concatenate([item_emb, item_cot], axis=1))
    user_first, item_first = run_section(first_users, first_items, None, None, user_degree, item_degree, tile_rows, tile_cols, tile_key, tile_count)
    user_layer = user_first[:, :EMB].astype(jnp.bfloat16)
    user_back = (user_cot.astype(jnp.float32) + user_first[:, EMB:]).astype(jnp.bfloat16)
    item_cot_blocks = to_column_blocks(item_cot)
    item_layer = item_first[..., :EMB].astype(jnp.bfloat16)
    item_back = (item_cot_blocks.astype(jnp.float32) + item_first[..., EMB:]).astype(jnp.bfloat16)
    later_users = jnp.concatenate([user_layer, user_back], axis=1)
    later_items = jnp.concatenate([item_layer, item_back], axis=-1)
    user_second, item_second = run_section(first_users, first_items, later_users, later_items, user_degree, item_degree, tile_rows, tile_cols, tile_key, tile_count)
    user_final = ((user_emb.astype(jnp.float32) + user_layer.astype(jnp.float32) + user_second[:, :EMB]) / 3.0).astype(jnp.bfloat16)
    user_grad = (user_cot.astype(jnp.float32) + user_second[:, EMB:]) / 3.0
    item_second_all = to_item_order(item_second)
    item_layer_all = to_item_order(item_layer)
    item_final = ((item_emb.astype(jnp.float32) + item_layer_all.astype(jnp.float32) + item_second_all[:, :EMB]) / 3.0).astype(jnp.bfloat16)
    item_grad = (item_cot.astype(jnp.float32) + item_second_all[:, EMB:]) / 3.0
    return (user_final, item_final, user_grad, item_grad)
```

```python
import functools

import jax
import jax.numpy as jnp
from jax import lax
from jax.experimental import pallas as pl
from jax.experimental.pallas import tpu as pltpu
from jax.sharding import PartitionSpec as P

EMB = 128
TILE = 256
MESH = pl.DeviceIdType.MESH
F32 = jnp.float32
BF16 = jnp.bfloat16


def nt_dot(left, right):
    return lax.dot_general(left, right, (((1,), (1,)), ((), ())), preferred_element_type=F32)


def nn_dot(left, right):
    return jnp.dot(left, right, preferred_element_type=F32)


def kernel(
    n_au,
    n_ia,
    keys,
    user_emb,
    item_emb,
    user_cot,
    item_cot,
    user_degree,
    item_degree,
    user_final,
    item_final,
    user_grad,
    item_grad,
    users,
    items,
    later_users,
    later_items,
    users_t,
    later_users_t,
    weight,
    adjacency,
    user_scale,
    item_scale,
    user_sum,
    item_sum,
    user_stage,
    item_stage,
    user_recv,
    item_recv,
    user_send_sem,
    user_recv_sem,
    item_send_sem,
    item_recv_sem,
):
    a = lax.axis_index("au")
    i = lax.axis_index("ia")
    us = user_emb.shape[0]
    it = item_emb.shape[0]
    u_block = us * n_ia
    i_block = it * n_au
    u_tiles = u_block // TILE
    i_tiles = i_block // TILE
    chunk = max(TILE, it)
    chunks = i_block // chunk
    chunk_tiles = chunk // TILE
    chunk_peers = chunk // it

    def rows(index, size):
        return pl.ds(pl.multiple_of(index * size, size), size)

    my_users = rows(i, us)
    my_items = rows(a, it)

    users[my_users, :EMB] = user_emb[...]
    users[my_users, EMB:] = user_cot[...]
    items[my_items, :EMB] = item_cot[...]
    items[my_items, EMB:] = item_emb[...]

    barrier = pltpu.get_barrier_semaphore()
    for d in range(1, n_ia):
        pl.semaphore_signal(barrier, inc=1, device_id=(a, lax.rem(i + d, n_ia)), device_id_type=MESH)
    for d in range(1, n_au):
        pl.semaphore_signal(barrier, inc=1, device_id=(lax.rem(a + d, n_au), i), device_id_type=MESH)
    pl.semaphore_wait(barrier, n_ia + n_au - 2)

    def spread_users(ref, phase, d):
        return pltpu.make_async_remote_copy(
            src_ref=ref.at[my_users],
            dst_ref=ref.at[my_users],
            send_sem=user_send_sem.at[phase, d],
            recv_sem=user_recv_sem.at[phase, d],
            device_id=(a, lax.rem(i + d, n_ia)),
            device_id_type=MESH,
        )

    def spread_items(ref, phase, d):
        return pltpu.make_async_remote_copy(
            src_ref=ref.at[my_items],
            dst_ref=ref.at[my_items],
            send_sem=item_send_sem.at[phase, d],
            recv_sem=item_recv_sem.at[phase, d],
            device_id=(lax.rem(a + d, n_au), i),
            device_id_type=MESH,
        )

    def user_part(layer, d):
        peer = lax.rem(i + d, n_ia)
        return pltpu.make_async_remote_copy(
            src_ref=user_stage.at[layer, rows(peer, us)],
            dst_ref=user_recv.at[layer, d],
            send_sem=user_send_sem.at[2 * layer + 1, d],
            recv_sem=user_recv_sem.at[2 * layer + 1, d],
            device_id=(a, peer),
            device_id_type=MESH,
        )

    def item_part(layer, d):
        peer = lax.rem(a + d, n_au)
        return pltpu.make_async_remote_copy(
            src_ref=item_stage.at[layer, rows(peer, it)],
            dst_ref=item_recv.at[layer, d],
            send_sem=item_send_sem.at[2 * layer + 1, d],
            recv_sem=item_recv_sem.at[2 * layer + 1, d],
            device_id=(peer, i),
            device_id_type=MESH,
        )

    for d in range(1, n_ia):
        spread_users(users, 0, d).start()
    for d in range(1, n_au):
        spread_items(items, 0, d).start()

    scale_row = lax.rsqrt(user_degree[...].astype(F32))
    for r in range(u_tiles):
        part = scale_row[:, r * TILE : (r + 1) * TILE]
        user_scale[r * TILE : (r + 1) * TILE, :] = jnp.transpose(
            jnp.broadcast_to(part, (128, TILE))
        )
    for p in range(n_au):
        item_scale[:, p * it : (p + 1) * it] = lax.rsqrt(item_degree[p].astype(F32))

    row_ids = lax.broadcasted_iota(jnp.int32, (TILE, 128), 0) * 977
    col_ids = lax.broadcasted_iota(jnp.int32, (1, TILE), 1) * 1531
    col_ids = lax.rem(col_ids, 8191) - 8191

    def fold(value):
        return (value & 8191) + (value >> 13)

    def mask_tile(t, carry):
        r = t // i_tiles
        c = t % i_tiles
        key = keys[t]
        target = jnp.where(key >= 0, 0, 8)
        h1 = fold(row_ids + key * 263)
        h1 = jnp.where(h1 >= 8191, h1 - 8191, h1)
        h1 = fold(h1 * h1)
        h1 = jnp.where(h1 >= 8191, h1 - 8191, h1)
        scale = user_scale[rows(r, TILE), :]
        for half in range(TILE // 128):
            lanes = slice(half * 128, (half + 1) * 128)
            h2 = h1 + col_ids[:, lanes]
            h3 = fold(h2 * h2)
            h3 = jnp.where(h3 >= 8191, h3 + 1, h3) & 7
            where = pl.ds(pl.multiple_of(c * TILE + half * 128, 128), 128)
            weight[rows(r, TILE), where] = jnp.where(
                h3 == target, scale * item_scale[:, where], 0.0
            )
        return carry

    lax.fori_loop(0, u_tiles * i_tiles, mask_tile, 0)

    user_sum[...] = jnp.zeros_like(user_sum)
    for d in range(1, n_ia):
        spread_users(users, 0, d).wait_recv()
    for r in range(u_tiles):
        users_t[:, r * TILE : (r + 1) * TILE] = jnp.transpose(users[r * TILE : (r + 1) * TILE, :])
    for d in range(1, n_au):
        spread_items(items, 0, d).wait_recv()

    def send_chunk(layer, k):
        for p in range(chunk_peers):
            peer = k * chunk_peers + p
            item_stage[layer, rows(peer, it), :] = jnp.transpose(
                item_sum[:, p * it : (p + 1) * it]
            ).astype(BF16)

            @pl.when(peer != a)
            def _():
                item_part(layer, lax.rem(peer - a + n_au, n_au)).start()

    def first_chunk(j, carry):
        k = lax.rem(a // chunk_peers + 1 + j, chunks)
        item_sum[...] = jnp.zeros_like(item_sum)

        def tile(t, inner):
            r = t // chunk_tiles
            c = t % chunk_tiles
            at_user = rows(r, TILE)
            at_item = rows(k * chunk_tiles + c, TILE)
            own_item = items[at_item, :]
            gate = jax.nn.sigmoid(nt_dot(users[at_user, :EMB], own_item[:, EMB:]))
            adj = gate * weight[at_user, at_item]
            weight[at_user, at_item] = adj * (1.0 - gate)
            adj = adj.astype(BF16)
            adjacency[at_user, at_item] = adj
            user_sum[at_user, :] += nn_dot(adj, own_item)
            item_sum[:, rows(c, TILE)] += nn_dot(users_t[:, at_user], adj)
            return inner

        lax.fori_loop(0, u_tiles * chunk_tiles, tile, 0)
        send_chunk(0, k)
        return carry

    lax.fori_loop(0, chunks, first_chunk, 0)

    user_stage[0] = user_sum[...].astype(BF16)
    for d in range(1, n_ia):
        user_part(0, d).start()

    def user_total(layer):
        total = user_stage[layer, my_users, :].astype(F32)
        for d in range(1, n_ia):
            user_part(layer, d).wait_recv()
            total = total + user_recv[layer, d].astype(F32)
        return total

    def item_total(layer):
        for d in range(1, n_au):
            item_part(layer, d).wait_recv()
        total = item_stage[layer, my_items, :].astype(F32)
        for d in range(1, n_au):
            total = total + item_recv[layer, d].astype(F32)
        return total

    total = item_total(0)
    later_items[my_items, :EMB] = (item_cot[...].astype(F32) + total[:, EMB:]).astype(BF16)
    later_items[my_items, EMB:] = total[:, :EMB].astype(BF16)
    for d in range(1, n_au):
        spread_items(later_items, 2, d).start()
    total = user_total(0)
    later_users[my_users, :EMB] = total[:, EMB:].astype(BF16)
    later_users[my_users, EMB:] = (user_cot[...].astype(F32) + total[:, :EMB]).astype(BF16)
    for d in range(1, n_ia):
        spread_users(later_users, 2, d).start()

    user_sum[...] = jnp.zeros_like(user_sum)
    for d in range(1, n_ia):
        spread_users(later_users, 2, d).wait_recv()
    for r in range(u_tiles):
        later_users_t[:, r * TILE : (r + 1) * TILE] = jnp.transpose(
            later_users[r * TILE : (r + 1) * TILE, :]
        )
    for d in range(1, n_au):
        spread_items(later_items, 2, d).wait_recv()

    def second_chunk(j, carry):
        k = lax.rem(a // chunk_peers + 1 + j, chunks)
        item_sum[...] = jnp.zeros_like(item_sum)

        def tile(t, inner):
            r = t // chunk_tiles
            c = t % chunk_tiles
            at_user = rows(r, TILE)
            at_item = rows(k * chunk_tiles + c, TILE)
            at_sum = rows(c, TILE)
            own_item = items[at_item, :]
            later_item = later_items[at_item, :]
            slope = nt_dot(users[at_user, :], later_item) + nt_dot(later_users[at_user, :], own_item)
            descent = (slope * weight[at_user, at_item]).astype(BF16)
            adj = adjacency[at_user, at_item]
            user_sum[at_user, :] += nn_dot(adj, later_item)
            user_sum[at_user, :EMB] += nn_dot(descent, own_item[:, EMB:])
            item_sum[:, at_sum] += nn_dot(later_users_t[:, at_user], adj)
            item_sum[EMB:, at_sum] += nn_dot(users_t[:EMB, at_user], descent)
            return inner

        lax.fori_loop(0, u_tiles * chunk_tiles, tile, 0)
        send_chunk(1, k)
        return carry

    lax.fori_loop(0, chunks, second_chunk, 0)

    user_stage[1] = user_sum[...].astype(BF16)
    for d in range(1, n_ia):
        user_part(1, d).start()

    total = item_total(1)
    layer = later_items[my_items, EMB:].astype(F32)
    item_final[...] = ((item_emb[...].astype(F32) + layer + total[:, :EMB]) / 3.0).astype(BF16)
    item_grad[...] = (item_cot[...].astype(F32) + total[:, EMB:]) / 3.0
    total = user_total(1)
    layer = later_users[my_users, :EMB].astype(F32)
    user_final[...] = ((user_emb[...].astype(F32) + layer + total[:, EMB:]) / 3.0).astype(BF16)
    user_grad[...] = (user_cot[...].astype(F32) + total[:, :EMB]) / 3.0

    for d in range(1, n_ia):
        spread_users(users, 0, d).wait_send()
        user_part(0, d).wait_send()
        spread_users(later_users, 2, d).wait_send()
        user_part(1, d).wait_send()
    for d in range(1, n_au):
        spread_items(items, 0, d).wait_send()
        item_part(0, d).wait_send()
        spread_items(later_items, 2, d).wait_send()
        item_part(1, d).wait_send()


def per_device(
    n_au,
    n_ia,
    user_emb,
    item_emb,
    user_cot,
    item_cot,
    user_degree,
    item_degree,
    tile_rows,
    tile_cols,
    tile_key,
    tile_count,
):
    us, it = user_emb.shape[0], item_emb.shape[0]
    u_block, i_block = us * n_ia, it * n_au
    u_tiles, i_tiles = u_block // TILE, i_block // TILE
    place = tile_rows.reshape(1, -1) * i_tiles + tile_cols.reshape(1, -1)
    slots = lax.broadcasted_iota(jnp.int32, place.shape, 1)
    place = jnp.where(slots < tile_count.reshape(1, 1), place, -1)
    found = place == lax.broadcasted_iota(jnp.int32, (u_tiles * i_tiles, 1), 0)
    keys = jnp.max(jnp.where(found, tile_key.reshape(1, -1), -1), axis=1)
    chunk = max(TILE, it)
    vmem = pl.BlockSpec(memory_space=pltpu.VMEM)
    smem = pl.BlockSpec(memory_space=pltpu.SMEM)
    return pl.pallas_call(
        functools.partial(kernel, n_au, n_ia),
        out_shape=(
            jax.ShapeDtypeStruct((us, EMB), BF16),
            jax.ShapeDtypeStruct((it, EMB), BF16),
            jax.ShapeDtypeStruct((us, EMB), F32),
            jax.ShapeDtypeStruct((it, EMB), F32),
        ),
        in_specs=[smem] + [vmem] * 6,
        out_specs=(vmem,) * 4,
        scratch_shapes=[
            pltpu.VMEM((u_block, 2 * EMB), BF16),
            pltpu.VMEM((i_block, 2 * EMB), BF16),
            pltpu.VMEM((u_block, 2 * EMB), BF16),
            pltpu.VMEM((i_block, 2 * EMB), BF16),
            pltpu.VMEM((2 * EMB, u_block), BF16),
            pltpu.VMEM((2 * EMB, u_block), BF16),
            pltpu.VMEM((u_block, i_block), F32),
            pltpu.VMEM((u_block, i_block), BF16),
            pltpu.VMEM((u_block, 128), F32),
            pltpu.VMEM((1, i_block), F32),
            pltpu.VMEM((u_block, 2 * EMB), F32),
            pltpu.VMEM((2 * EMB, chunk), F32),
            pltpu.VMEM((2, u_block, 2 * EMB), BF16),
            pltpu.VMEM((2, i_block, 2 * EMB), BF16),
            pltpu.VMEM((2, n_ia, us, 2 * EMB), BF16),
            pltpu.VMEM((2, n_au, it, 2 * EMB), BF16),
            pltpu.SemaphoreType.DMA((4, n_ia)),
            pltpu.SemaphoreType.DMA((4, n_ia)),
            pltpu.SemaphoreType.DMA((4, n_au)),
            pltpu.SemaphoreType.DMA((4, n_au)),
        ],
        compiler_params=pltpu.CompilerParams(
            collective_id=0, has_side_effects=True, vmem_limit_bytes=48 * 1024 * 1024
        ),
    )(
        keys,
        user_emb,
        item_emb,
        user_cot,
        item_cot,
        user_degree.reshape(1, -1),
        item_degree,
    )


def solution(mesh):
    shards = P(("au", "ia"), None)
    in_specs = (
        shards,
        shards,
        shards,
        shards,
        P("au"),
        P(None, "ia", None),
        P("au", "ia", None),
        P("au", "ia", None),
        P("au", "ia", None),
        P("au", "ia"),
    )
    return jax.shard_map(
        functools.partial(per_device, mesh.shape["au"], mesh.shape["ia"]),
        mesh=mesh,
        in_specs=in_specs,
        out_specs=(shards,) * 4,
        check_vma=False,
    )
```

```python
import functools

import jax
import jax.numpy as jnp
from jax import lax
from jax.experimental import pallas as pl
from jax.experimental.pallas import tpu as pltpu
from jax.sharding import PartitionSpec as P

EMB = 128
TILE = 256
MESH = pl.DeviceIdType.MESH
F32 = jnp.float32
BF16 = jnp.bfloat16


def nt_dot(left, right):
    return lax.dot_general(left, right, (((1,), (1,)), ((), ())), preferred_element_type=F32)


def nn_dot(left, right):
    return jnp.dot(left, right, preferred_element_type=F32)


def kernel(
    n_au,
    n_ia,
    user_emb,
    item_emb,
    user_cot,
    item_cot,
    user_degree_hbm,
    item_degree_hbm,
    tile_rows_hbm,
    tile_cols_hbm,
    tile_key_hbm,
    tile_count_hbm,
    user_final,
    item_final,
    user_grad,
    item_grad,
    users,
    items,
    later_users,
    later_items,
    users_t,
    later_users_t,
    weight,
    adjacency,
    user_scale,
    item_scale,
    user_sum,
    item_sum,
    user_stage,
    item_stage,
    user_pair,
    user_send,
    user_recv,
    item_recv,
    user_degree,
    item_degree,
    tile_rows,
    tile_cols,
    tile_key,
    tile_count,
    local_sem,
    user_send_sem,
    user_recv_sem,
    item_send_sem,
    item_recv_sem,
):
    a = lax.axis_index("au")
    i = lax.axis_index("ia")
    us = user_emb.shape[0]
    it = item_emb.shape[0]
    u_block = us * n_ia
    i_block = it * n_au
    u_tiles = u_block // TILE
    i_tiles = i_block // TILE
    chunk = max(TILE, it)
    chunks = i_block // chunk
    chunk_tiles = chunk // TILE
    chunk_peers = chunk // it

    def rows(index, size):
        return pl.ds(pl.multiple_of(index * size, size), size)

    my_users = rows(i, us)
    my_items = rows(a, it)

    local = [
        pltpu.make_async_copy(src, dst, local_sem.at[n])
        for n, (src, dst) in enumerate(
            (
                (user_emb, users.at[my_users, :EMB]),
                (user_cot, users.at[my_users, EMB:]),
                (item_cot, items.at[my_items, :EMB]),
                (item_emb, items.at[my_items, EMB:]),
                (user_degree_hbm, user_degree),
                (item_degree_hbm, item_degree),
                (tile_rows_hbm, tile_rows),
                (tile_cols_hbm, tile_cols),
                (tile_key_hbm, tile_key),
                (tile_count_hbm, tile_count),
            )
        )
    ]
    for copy in local:
        copy.start()

    nz = n_ia // 2
    sibling = i + 1 - 2 * lax.rem(i, 2)

    barrier = pltpu.get_barrier_semaphore()
    pl.semaphore_signal(barrier, inc=1, device_id=(a, sibling), device_id_type=MESH)
    for e in range(1, nz):
        pl.semaphore_signal(
            barrier, inc=1, device_id=(a, lax.rem(i + 2 * e, n_ia)), device_id_type=MESH
        )
    for d in range(1, n_au):
        pl.semaphore_signal(barrier, inc=1, device_id=(lax.rem(a + d, n_au), i), device_id_type=MESH)
    pl.semaphore_wait(barrier, nz + n_au - 1)

    def user_copy(src, dst, phase, d, peer):
        return pltpu.make_async_remote_copy(
            src_ref=src,
            dst_ref=dst,
            send_sem=user_send_sem.at[phase, d],
            recv_sem=user_recv_sem.at[phase, d],
            device_id=(a, peer),
            device_id_type=MESH,
        )

    def spread_along(ref, phase, e):
        part = ref.at[my_users]
        return user_copy(part, part, phase, 2 * e, lax.rem(i + 2 * e, n_ia))

    def spread_across(ref, phase, e):
        part = ref.at[rows(lax.rem(i + n_ia - 2 * e, n_ia), us)]
        return user_copy(part, part, phase, 2 * e + 1, sibling)

    def spread_start(ref, phase):
        for e in range(1, nz):
            spread_along(ref, phase, e).start()
        spread_across(ref, phase, 0).start()

    def spread_forward(ref, phase):
        for e in range(1, nz):
            spread_along(ref, phase, e).wait_recv()
            spread_across(ref, phase, e).start()

    def spread_end(ref, phase):
        for e in range(nz):
            spread_across(ref, phase, e).wait_recv()

    def spread_items(ref, phase, d):
        return pltpu.make_async_remote_copy(
            src_ref=ref.at[my_items],
            dst_ref=ref.at[my_items],
            send_sem=item_send_sem.at[phase, d],
            recv_sem=item_recv_sem.at[phase, d],
            device_id=(lax.rem(a + d, n_au), i),
            device_id_type=MESH,
        )

    def pair_part(layer, e):
        owner = lax.rem(sibling + 2 * e, n_ia)
        return user_copy(
            user_stage.at[layer, rows(owner, us)],
            user_pair.at[layer, e],
            2 * layer + 1,
            2 * e + 1,
            sibling,
        )

    def user_part(layer, e):
        return user_copy(
            user_send.at[layer, e],
            user_recv.at[layer, e],
            2 * layer + 1,
            2 * e,
            lax.rem(i + 2 * e, n_ia),
        )

    def send_users(layer):
        user_stage[layer] = user_sum[...].astype(BF16)
        order = list(range(1, nz)) + [0]
        for e in order:
            pair_part(layer, e).start()
        for e in order:
            pair_part(layer, e).wait_recv()
            if e:
                own = user_stage[layer, rows(lax.rem(i + 2 * e, n_ia), us), :].astype(F32)
                user_send[layer, e] = (own + user_pair[layer, e].astype(F32)).astype(BF16)
                user_part(layer, e).start()

    def item_part(layer, d):
        peer = lax.rem(a + d, n_au)
        return pltpu.make_async_remote_copy(
            src_ref=item_stage.at[layer, rows(peer, it)],
            dst_ref=item_recv.at[layer, d],
            send_sem=item_send_sem.at[2 * layer + 1, d],
            recv_sem=item_recv_sem.at[2 * layer + 1, d],
            device_id=(peer, i),
            device_id_type=MESH,
        )

    for copy in local:
        copy.wait()
    spread_start(users, 0)
    for d in range(1, n_au):
        spread_items(items, 0, d).start()

    slots = lax.broadcasted_iota(jnp.int32, tile_key.shape, 1)
    places = jnp.where(slots < tile_count[...], tile_rows[...] * i_tiles + tile_cols[...], -1)
    slot_keys = tile_key[...]

    scale_row = lax.rsqrt(user_degree[...].astype(F32))
    for r in range(u_tiles):
        part = scale_row[:, r * TILE : (r + 1) * TILE]
        user_scale[r * TILE : (r + 1) * TILE, :] = jnp.transpose(
            jnp.broadcast_to(part, (128, TILE))
        )
    for p in range(n_au):
        item_scale[:, p * it : (p + 1) * it] = lax.rsqrt(item_degree[p].astype(F32))

    row_ids = lax.broadcasted_iota(jnp.int32, (TILE, 128), 0) * 977
    col_ids = lax.broadcasted_iota(jnp.int32, (1, TILE), 1) * 1531
    col_ids = lax.rem(col_ids, 8191) - 8191

    def fold(value):
        return (value & 8191) + (value >> 13)

    def mask_tile(t, carry):
        r = t // i_tiles
        c = t % i_tiles
        key = jnp.max(jnp.where(places == t, slot_keys, -1), axis=1, keepdims=True)
        target = jnp.where(key >= 0, 0, 8)
        h1 = fold(row_ids + key * 263)
        h1 = jnp.where(h1 >= 8191, h1 - 8191, h1)
        h1 = fold(h1 * h1)
        h1 = jnp.where(h1 >= 8191, h1 - 8191, h1)
        scale = user_scale[rows(r, TILE), :]
        for half in range(TILE // 128):
            lanes = slice(half * 128, (half + 1) * 128)
            h2 = h1 + col_ids[:, lanes]
            h3 = fold(h2 * h2)
            h3 = jnp.where(h3 >= 8191, h3 + 1, h3) & 7
            where = pl.ds(pl.multiple_of(c * TILE + half * 128, 128), 128)
            weight[rows(r, TILE), where] = jnp.where(
                h3 == target, scale * item_scale[:, where], 0.0
            )
        return carry

    tiles = u_tiles * i_tiles
    lax.fori_loop(0, tiles // 2, mask_tile, 0)
    spread_forward(users, 0)
    lax.fori_loop(tiles // 2, tiles, mask_tile, 0)

    user_sum[...] = jnp.zeros_like(user_sum)
    spread_end(users, 0)
    for r in range(u_tiles):
        users_t[:, r * TILE : (r + 1) * TILE] = jnp.transpose(users[r * TILE : (r + 1) * TILE, :])
    for d in range(1, n_au):
        spread_items(items, 0, d).wait_recv()

    def send_chunk(layer, k):
        for p in range(chunk_peers):
            peer = k * chunk_peers + p
            item_stage[layer, rows(peer, it), :] = jnp.transpose(
                item_sum[:, p * it : (p + 1) * it]
            ).astype(BF16)

            @pl.when(peer != a)
            def _():
                item_part(layer, lax.rem(peer - a + n_au, n_au)).start()

    def first_chunk(j, carry):
        k = lax.rem(a // chunk_peers + 1 + j, chunks)
        item_sum[...] = jnp.zeros_like(item_sum)

        def tile(t, inner):
            r = t // chunk_tiles
            c = t % chunk_tiles
            at_user = rows(r, TILE)
            at_item = rows(k * chunk_tiles + c, TILE)
            own_item = items[at_item, :]
            gate = jax.nn.sigmoid(nt_dot(users[at_user, :EMB], own_item[:, EMB:]))
            adj = gate * weight[at_user, at_item]
            weight[at_user, at_item] = adj * (1.0 - gate)
            adj = adj.astype(BF16)
            adjacency[at_user, at_item] = adj
            user_sum[at_user, :] += nn_dot(adj, own_item)
            item_sum[:, rows(c, TILE)] += nn_dot(users_t[:, at_user], adj)
            return inner

        lax.fori_loop(0, u_tiles * chunk_tiles, tile, 0, unroll=4)
        send_chunk(0, k)
        return carry

    lax.fori_loop(0, chunks, first_chunk, 0)

    send_users(0)

    def user_total(layer):
        total = user_stage[layer, my_users, :].astype(F32) + user_pair[layer, 0].astype(F32)
        for e in range(1, nz):
            user_part(layer, e).wait_recv()
            total = total + user_recv[layer, e].astype(F32)
        return total

    def item_total(layer):
        for d in range(1, n_au):
            item_part(layer, d).wait_recv()
        total = item_stage[layer, my_items, :].astype(F32)
        for d in range(1, n_au):
            total = total + item_recv[layer, d].astype(F32)
        return total

    total = item_total(0)
    later_items[my_items, :EMB] = (items[my_items, :EMB].astype(F32) + total[:, EMB:]).astype(BF16)
    later_items[my_items, EMB:] = total[:, :EMB].astype(BF16)
    for d in range(1, n_au):
        spread_items(later_items, 2, d).start()
    total = user_total(0)
    later_users[my_users, :EMB] = total[:, EMB:].astype(BF16)
    later_users[my_users, EMB:] = (users[my_users, EMB:].astype(F32) + total[:, :EMB]).astype(BF16)
    spread_start(later_users, 2)

    user_sum[...] = jnp.zeros_like(user_sum)
    spread_forward(later_users, 2)
    spread_end(later_users, 2)
    for r in range(u_tiles):
        later_users_t[:, r * TILE : (r + 1) * TILE] = jnp.transpose(
            later_users[r * TILE : (r + 1) * TILE, :]
        )
    for d in range(1, n_au):
        spread_items(later_items, 2, d).wait_recv()

    def second_chunk(j, carry):
        k = lax.rem(a // chunk_peers + 1 + j, chunks)
        item_sum[...] = jnp.zeros_like(item_sum)

        def tile(t, inner):
            r = t // chunk_tiles
            c = t % chunk_tiles
            at_user = rows(r, TILE)
            at_item = rows(k * chunk_tiles + c, TILE)
            at_sum = rows(c, TILE)
            own_item = items[at_item, :]
            later_item = later_items[at_item, :]
            slope = nt_dot(users[at_user, :], later_item) + nt_dot(later_users[at_user, :], own_item)
            descent = (slope * weight[at_user, at_item]).astype(BF16)
            adj = adjacency[at_user, at_item]
            user_sum[at_user, :] += nn_dot(adj, later_item)
            user_sum[at_user, :EMB] += nn_dot(descent, own_item[:, EMB:])
            item_sum[:, at_sum] += nn_dot(later_users_t[:, at_user], adj)
            item_sum[EMB:, at_sum] += nn_dot(users_t[:EMB, at_user], descent)
            return inner

        lax.fori_loop(0, u_tiles * chunk_tiles, tile, 0, unroll=4)
        send_chunk(1, k)
        return carry

    lax.fori_loop(0, chunks, second_chunk, 0)

    send_users(1)

    total = item_total(1)
    layer = later_items[my_items, EMB:].astype(F32)
    item_final[...] = ((items[my_items, EMB:].astype(F32) + layer + total[:, :EMB]) / 3.0).astype(BF16)
    item_grad[...] = (items[my_items, :EMB].astype(F32) + total[:, EMB:]) / 3.0
    total = user_total(1)
    layer = later_users[my_users, :EMB].astype(F32)
    user_final[...] = ((users[my_users, :EMB].astype(F32) + layer + total[:, EMB:]) / 3.0).astype(BF16)
    user_grad[...] = (users[my_users, EMB:].astype(F32) + total[:, :EMB]) / 3.0

    for e in range(nz):
        spread_across(users, 0, e).wait_send()
        spread_across(later_users, 2, e).wait_send()
        pair_part(0, e).wait_send()
        pair_part(1, e).wait_send()
    for e in range(1, nz):
        spread_along(users, 0, e).wait_send()
        spread_along(later_users, 2, e).wait_send()
        user_part(0, e).wait_send()
        user_part(1, e).wait_send()
    for d in range(1, n_au):
        spread_items(items, 0, d).wait_send()
        item_part(0, d).wait_send()
        spread_items(later_items, 2, d).wait_send()
        item_part(1, d).wait_send()


def per_device(
    n_au,
    n_ia,
    user_emb,
    item_emb,
    user_cot,
    item_cot,
    user_degree,
    item_degree,
    tile_rows,
    tile_cols,
    tile_key,
    tile_count,
):
    us, it = user_emb.shape[0], item_emb.shape[0]
    u_block, i_block = us * n_ia, it * n_au
    chunk = max(TILE, it)
    vmem = pl.BlockSpec(memory_space=pltpu.VMEM)
    slots = tile_key.shape[-1]
    return pl.pallas_call(
        functools.partial(kernel, n_au, n_ia),
        out_shape=(
            jax.ShapeDtypeStruct((us, EMB), BF16),
            jax.ShapeDtypeStruct((it, EMB), BF16),
            jax.ShapeDtypeStruct((us, EMB), F32),
            jax.ShapeDtypeStruct((it, EMB), F32),
        ),
        in_specs=[pl.BlockSpec(memory_space=pl.ANY)] * 10,
        out_specs=(vmem,) * 4,
        scratch_shapes=[
            pltpu.VMEM((u_block, 2 * EMB), BF16),
            pltpu.VMEM((i_block, 2 * EMB), BF16),
            pltpu.VMEM((u_block, 2 * EMB), BF16),
            pltpu.VMEM((i_block, 2 * EMB), BF16),
            pltpu.VMEM((2 * EMB, u_block), BF16),
            pltpu.VMEM((2 * EMB, u_block), BF16),
            pltpu.VMEM((u_block, i_block), F32),
            pltpu.VMEM((u_block, i_block), BF16),
            pltpu.VMEM((u_block, 128), F32),
            pltpu.VMEM((1, i_block), F32),
            pltpu.VMEM((u_block, 2 * EMB), F32),
            pltpu.VMEM((2 * EMB, chunk), F32),
            pltpu.VMEM((2, u_block, 2 * EMB), BF16),
            pltpu.VMEM((2, i_block, 2 * EMB), BF16),
            pltpu.VMEM((2, n_ia // 2, us, 2 * EMB), BF16),
            pltpu.VMEM((2, n_ia // 2, us, 2 * EMB), BF16),
            pltpu.VMEM((2, n_ia // 2, us, 2 * EMB), BF16),
            pltpu.VMEM((2, n_au, it, 2 * EMB), BF16),
            pltpu.VMEM((1, u_block), jnp.int32),
            pltpu.VMEM((n_au, 1, it), jnp.int32),
            pltpu.VMEM((1, slots), jnp.int32),
            pltpu.VMEM((1, slots), jnp.int32),
            pltpu.VMEM((1, slots), jnp.int32),
            pltpu.VMEM((1, 1), jnp.int32),
            pltpu.SemaphoreType.DMA((10,)),
            pltpu.SemaphoreType.DMA((4, n_ia)),
            pltpu.SemaphoreType.DMA((4, n_ia)),
            pltpu.SemaphoreType.DMA((4, n_au)),
            pltpu.SemaphoreType.DMA((4, n_au)),
        ],
        compiler_params=pltpu.CompilerParams(
            collective_id=0, has_side_effects=True, vmem_limit_bytes=48 * 1024 * 1024
        ),
    )(
        user_emb,
        item_emb,
        user_cot,
        item_cot,
        user_degree.reshape(1, -1),
        item_degree,
        tile_rows.reshape(1, -1),
        tile_cols.reshape(1, -1),
        tile_key.reshape(1, -1),
        tile_count,
    )


def solution(mesh):
    shards = P(("au", "ia"), None)
    in_specs = (
        shards,
        shards,
        shards,
        shards,
        P("au"),
        P(None, "ia", None),
        P("au", "ia", None),
        P("au", "ia", None),
        P("au", "ia", None),
        P("au", "ia"),
    )
    return jax.shard_map(
        functools.partial(per_device, mesh.shape["au"], mesh.shape["ia"]),
        mesh=mesh,
        in_specs=in_specs,
        out_specs=(shards,) * 4,
        check_vma=False,
    )
```

```python
import functools

import jax
import jax.numpy as jnp
from jax import lax
from jax.experimental import pallas as pl
from jax.experimental.pallas import tpu as pltpu
from jax.sharding import PartitionSpec as P

EMB = 128
TILE = 256
MESH = pl.DeviceIdType.MESH
F32 = jnp.float32
BF16 = jnp.bfloat16


def nt_dot(left, right):
    return lax.dot_general(left, right, (((1,), (1,)), ((), ())), preferred_element_type=F32)


def nn_dot(left, right):
    return jnp.dot(left, right, preferred_element_type=F32)


def kernel(
    n_au,
    n_ia,
    user_emb,
    item_emb,
    user_cot,
    item_cot,
    user_degree_hbm,
    item_degree_hbm,
    tile_rows_hbm,
    tile_cols_hbm,
    tile_key_hbm,
    tile_count_hbm,
    user_final,
    item_final,
    user_grad,
    item_grad,
    users,
    items,
    later_users,
    later_items,
    users_t,
    later_users_t,
    weight,
    adjacency,
    user_scale,
    item_scale,
    user_sum,
    item_sum,
    user_stage,
    item_stage,
    user_pair,
    user_send,
    user_recv,
    item_recv,
    user_degree,
    item_degree,
    tile_rows,
    tile_cols,
    tile_key,
    tile_count,
    local_sem,
    user_send_sem,
    user_recv_sem,
    item_send_sem,
    item_recv_sem,
):
    a = lax.axis_index("au")
    i = lax.axis_index("ia")
    us = user_emb.shape[0]
    it = item_emb.shape[0]
    u_block = us * n_ia
    i_block = it * n_au
    u_tiles = u_block // TILE
    i_tiles = i_block // TILE
    chunk = max(TILE, it)
    chunks = i_block // chunk
    chunk_tiles = chunk // TILE
    chunk_peers = chunk // it

    def rows(index, size):
        return pl.ds(pl.multiple_of(index * size, size), size)

    my_users = rows(i, us)
    my_items = rows(a, it)

    local = [
        pltpu.make_async_copy(src, dst, local_sem.at[n])
        for n, (src, dst) in enumerate(
            (
                (user_emb, users.at[my_users, :EMB]),
                (user_cot, users.at[my_users, EMB:]),
                (item_cot, items.at[my_items, :EMB]),
                (item_emb, items.at[my_items, EMB:]),
                (user_degree_hbm, user_degree),
                (item_degree_hbm, item_degree),
                (tile_rows_hbm, tile_rows),
                (tile_cols_hbm, tile_cols),
                (tile_key_hbm, tile_key),
                (tile_count_hbm, tile_count),
            )
        )
    ]
    for copy in local:
        copy.start()

    nz = n_ia // 2
    sibling = i + 1 - 2 * lax.rem(i, 2)

    barrier = pltpu.get_barrier_semaphore()
    pl.semaphore_signal(barrier, inc=1, device_id=(a, sibling), device_id_type=MESH)
    for e in range(1, nz):
        pl.semaphore_signal(
            barrier, inc=1, device_id=(a, lax.rem(i + 2 * e, n_ia)), device_id_type=MESH
        )
    for d in range(1, n_au):
        pl.semaphore_signal(barrier, inc=1, device_id=(lax.rem(a + d, n_au), i), device_id_type=MESH)
    pl.semaphore_wait(barrier, nz + n_au - 1)

    def user_copy(src, dst, phase, d, peer):
        return pltpu.make_async_remote_copy(
            src_ref=src,
            dst_ref=dst,
            send_sem=user_send_sem.at[phase, d],
            recv_sem=user_recv_sem.at[phase, d],
            device_id=(a, peer),
            device_id_type=MESH,
        )

    def spread_along(ref, phase, e):
        part = ref.at[my_users]
        return user_copy(part, part, phase, 2 * e, lax.rem(i + 2 * e, n_ia))

    def spread_across(ref, phase, e):
        part = ref.at[rows(lax.rem(i + n_ia - 2 * e, n_ia), us)]
        return user_copy(part, part, phase, 2 * e + 1, sibling)

    def spread_start(ref, phase):
        for e in range(1, nz):
            spread_along(ref, phase, e).start()
        spread_across(ref, phase, 0).start()

    def spread_forward(ref, phase):
        for e in range(1, nz):
            spread_along(ref, phase, e).wait_recv()
            spread_across(ref, phase, e).start()

    def spread_end(ref, phase):
        for e in range(nz):
            spread_across(ref, phase, e).wait_recv()

    def spread_items(ref, phase, d):
        return pltpu.make_async_remote_copy(
            src_ref=ref.at[my_items],
            dst_ref=ref.at[my_items],
            send_sem=item_send_sem.at[phase, d],
            recv_sem=item_recv_sem.at[phase, d],
            device_id=(lax.rem(a + d, n_au), i),
            device_id_type=MESH,
        )

    def pair_part(layer, e):
        owner = lax.rem(sibling + 2 * e, n_ia)
        return user_copy(
            user_stage.at[layer, rows(owner, us)],
            user_pair.at[layer, e],
            2 * layer + 1,
            2 * e + 1,
            sibling,
        )

    def user_part(layer, e):
        return user_copy(
            user_send.at[layer, e],
            user_recv.at[layer, e],
            2 * layer + 1,
            2 * e,
            lax.rem(i + 2 * e, n_ia),
        )

    def send_users(layer):
        user_stage[layer] = user_sum[...].astype(BF16)
        order = list(range(1, nz)) + [0]
        for e in order:
            pair_part(layer, e).start()
        for e in order:
            pair_part(layer, e).wait_recv()
            if e:
                own = user_stage[layer, rows(lax.rem(i + 2 * e, n_ia), us), :].astype(F32)
                user_send[layer, e] = (own + user_pair[layer, e].astype(F32)).astype(BF16)
                user_part(layer, e).start()

    def item_part(layer, d):
        peer = lax.rem(a + d, n_au)
        return pltpu.make_async_remote_copy(
            src_ref=item_stage.at[layer, rows(peer, it)],
            dst_ref=item_recv.at[layer, d],
            send_sem=item_send_sem.at[2 * layer + 1, d],
            recv_sem=item_recv_sem.at[2 * layer + 1, d],
            device_id=(peer, i),
            device_id_type=MESH,
        )

    for copy in local:
        copy.wait()
    spread_start(users, 0)
    for d in reversed(range(1, n_au)):
        spread_items(items, 0, d).start()

    slots = lax.broadcasted_iota(jnp.int32, tile_key.shape, 1)
    places = jnp.where(slots < tile_count[...], tile_rows[...] * i_tiles + tile_cols[...], -1)
    slot_keys = tile_key[...]

    scale_row = lax.rsqrt(user_degree[...].astype(F32))
    for r in range(u_tiles):
        part = scale_row[:, r * TILE : (r + 1) * TILE]
        user_scale[r * TILE : (r + 1) * TILE, :] = jnp.transpose(
            jnp.broadcast_to(part, (128, TILE))
        )
    for p in range(n_au):
        item_scale[:, p * it : (p + 1) * it] = lax.rsqrt(item_degree[p].astype(F32))

    row_ids = lax.broadcasted_iota(jnp.int32, (TILE, 128), 0) * 977
    col_ids = lax.broadcasted_iota(jnp.int32, (1, TILE), 1) * 1531
    col_ids = lax.rem(col_ids, 8191) - 8191

    def fold(value):
        return (value & 8191) + (value >> 13)

    def mask_tile(t, carry):
        r = t // i_tiles
        c = t % i_tiles
        key = jnp.max(jnp.where(places == t, slot_keys, -1), axis=1, keepdims=True)
        target = jnp.where(key >= 0, 0, 8)
        h1 = fold(row_ids + key * 263)
        h1 = jnp.where(h1 >= 8191, h1 - 8191, h1)
        h1 = fold(h1 * h1)
        h1 = jnp.where(h1 >= 8191, h1 - 8191, h1)
        scale = user_scale[rows(r, TILE), :]
        for half in range(TILE // 128):
            lanes = slice(half * 128, (half + 1) * 128)
            h2 = h1 + col_ids[:, lanes]
            h3 = fold(h2 * h2)
            h3 = jnp.where(h3 >= 8191, h3 + 1, h3) & 7
            where = pl.ds(pl.multiple_of(c * TILE + half * 128, 128), 128)
            weight[rows(r, TILE), where] = jnp.where(
                h3 == target, scale * item_scale[:, where], 0.0
            )
        return carry

    tiles = u_tiles * i_tiles
    lax.fori_loop(0, tiles // 2, mask_tile, 0)
    spread_forward(users, 0)
    lax.fori_loop(tiles // 2, tiles, mask_tile, 0)

    user_sum[...] = jnp.zeros_like(user_sum)
    spread_end(users, 0)
    for r in range(u_tiles):
        users_t[:, r * TILE : (r + 1) * TILE] = jnp.transpose(users[r * TILE : (r + 1) * TILE, :])

    def await_chunk(ref, phase, k):
        for p in range(chunk_peers):
            d = lax.rem(a - k * chunk_peers - p + n_au, n_au)

            @pl.when(d != 0)
            def _():
                spread_items(ref, phase, d).wait_recv()

    def send_chunk(layer, k):
        for p in range(chunk_peers):
            peer = k * chunk_peers + p
            item_stage[layer, rows(peer, it), :] = jnp.transpose(
                item_sum[:, p * it : (p + 1) * it]
            ).astype(BF16)

            @pl.when(peer != a)
            def _():
                item_part(layer, lax.rem(peer - a + n_au, n_au)).start()

    def first_chunk(j, carry):
        k = lax.rem(a // chunk_peers + 1 + j, chunks)
        await_chunk(items, 0, k)
        item_sum[...] = jnp.zeros_like(item_sum)

        def tile(t, inner):
            r = t // chunk_tiles
            c = t % chunk_tiles
            at_user = rows(r, TILE)
            at_item = rows(k * chunk_tiles + c, TILE)
            own_item = items[at_item, :]
            gate = jax.nn.sigmoid(nt_dot(users[at_user, :EMB], own_item[:, EMB:]))
            adj = gate * weight[at_user, at_item]
            weight[at_user, at_item] = adj * (1.0 - gate)
            adj = adj.astype(BF16)
            adjacency[at_user, at_item] = adj
            user_sum[at_user, :] += nn_dot(adj, own_item)
            item_sum[:, rows(c, TILE)] += nn_dot(users_t[:, at_user], adj)
            return inner

        lax.fori_loop(0, u_tiles * chunk_tiles, tile, 0, unroll=4)
        send_chunk(0, k)
        return carry

    lax.fori_loop(0, chunks, first_chunk, 0)

    send_users(0)

    def user_total(layer):
        total = user_stage[layer, my_users, :].astype(F32) + user_pair[layer, 0].astype(F32)
        for e in range(1, nz):
            user_part(layer, e).wait_recv()
            total = total + user_recv[layer, e].astype(F32)
        return total

    def item_total(layer):
        for d in range(1, n_au):
            item_part(layer, d).wait_recv()
        total = item_stage[layer, my_items, :].astype(F32)
        for d in range(1, n_au):
            total = total + item_recv[layer, d].astype(F32)
        return total

    total = item_total(0)
    later_items[my_items, :EMB] = (items[my_items, :EMB].astype(F32) + total[:, EMB:]).astype(BF16)
    later_items[my_items, EMB:] = total[:, :EMB].astype(BF16)
    for d in reversed(range(1, n_au)):
        spread_items(later_items, 2, d).start()
    total = user_total(0)
    later_users[my_users, :EMB] = total[:, EMB:].astype(BF16)
    later_users[my_users, EMB:] = (users[my_users, EMB:].astype(F32) + total[:, :EMB]).astype(BF16)
    spread_start(later_users, 2)

    user_sum[...] = jnp.zeros_like(user_sum)
    spread_forward(later_users, 2)
    spread_end(later_users, 2)
    for r in range(u_tiles):
        later_users_t[:, r * TILE : (r + 1) * TILE] = jnp.transpose(
            later_users[r * TILE : (r + 1) * TILE, :]
        )

    def second_chunk(j, carry):
        k = lax.rem(a // chunk_peers + 1 + j, chunks)
        await_chunk(later_items, 2, k)
        item_sum[...] = jnp.zeros_like(item_sum)

        def tile(t, inner):
            r = t // chunk_tiles
            c = t % chunk_tiles
            at_user = rows(r, TILE)
            at_item = rows(k * chunk_tiles + c, TILE)
            at_sum = rows(c, TILE)
            own_item = items[at_item, :]
            later_item = later_items[at_item, :]
            slope = nt_dot(users[at_user, :], later_item) + nt_dot(later_users[at_user, :], own_item)
            descent = (slope * weight[at_user, at_item]).astype(BF16)
            adj = adjacency[at_user, at_item]
            user_sum[at_user, :] += nn_dot(adj, later_item)
            user_sum[at_user, :EMB] += nn_dot(descent, own_item[:, EMB:])
            item_sum[:, at_sum] += nn_dot(later_users_t[:, at_user], adj)
            item_sum[EMB:, at_sum] += nn_dot(users_t[:EMB, at_user], descent)
            return inner

        lax.fori_loop(0, u_tiles * chunk_tiles, tile, 0, unroll=4)
        send_chunk(1, k)
        return carry

    lax.fori_loop(0, chunks, second_chunk, 0)

    send_users(1)

    total = item_total(1)
    layer = later_items[my_items, EMB:].astype(F32)
    item_final[...] = ((items[my_items, EMB:].astype(F32) + layer + total[:, :EMB]) / 3.0).astype(BF16)
    item_grad[...] = (items[my_items, :EMB].astype(F32) + total[:, EMB:]) / 3.0
    total = user_total(1)
    layer = later_users[my_users, :EMB].astype(F32)
    user_final[...] = ((users[my_users, :EMB].astype(F32) + layer + total[:, EMB:]) / 3.0).astype(BF16)
    user_grad[...] = (users[my_users, EMB:].astype(F32) + total[:, :EMB]) / 3.0

    for e in range(nz):
        spread_across(users, 0, e).wait_send()
        spread_across(later_users, 2, e).wait_send()
        pair_part(0, e).wait_send()
        pair_part(1, e).wait_send()
    for e in range(1, nz):
        spread_along(users, 0, e).wait_send()
        spread_along(later_users, 2, e).wait_send()
        user_part(0, e).wait_send()
        user_part(1, e).wait_send()
    for d in range(1, n_au):
        spread_items(items, 0, d).wait_send()
        item_part(0, d).wait_send()
        spread_items(later_items, 2, d).wait_send()
        item_part(1, d).wait_send()


def per_device(
    n_au,
    n_ia,
    user_emb,
    item_emb,
    user_cot,
    item_cot,
    user_degree,
    item_degree,
    tile_rows,
    tile_cols,
    tile_key,
    tile_count,
):
    us, it = user_emb.shape[0], item_emb.shape[0]
    u_block, i_block = us * n_ia, it * n_au
    chunk = max(TILE, it)
    vmem = pl.BlockSpec(memory_space=pltpu.VMEM)
    slots = tile_key.shape[-1]
    return pl.pallas_call(
        functools.partial(kernel, n_au, n_ia),
        out_shape=(
            jax.ShapeDtypeStruct((us, EMB), BF16),
            jax.ShapeDtypeStruct((it, EMB), BF16),
            jax.ShapeDtypeStruct((us, EMB), F32),
            jax.ShapeDtypeStruct((it, EMB), F32),
        ),
        in_specs=[pl.BlockSpec(memory_space=pl.ANY)] * 10,
        out_specs=(vmem,) * 4,
        scratch_shapes=[
            pltpu.VMEM((u_block, 2 * EMB), BF16),
            pltpu.VMEM((i_block, 2 * EMB), BF16),
            pltpu.VMEM((u_block, 2 * EMB), BF16),
            pltpu.VMEM((i_block, 2 * EMB), BF16),
            pltpu.VMEM((2 * EMB, u_block), BF16),
            pltpu.VMEM((2 * EMB, u_block), BF16),
            pltpu.VMEM((u_block, i_block), F32),
            pltpu.VMEM((u_block, i_block), BF16),
            pltpu.VMEM((u_block, 128), F32),
            pltpu.VMEM((1, i_block), F32),
            pltpu.VMEM((u_block, 2 * EMB), F32),
            pltpu.VMEM((2 * EMB, chunk), F32),
            pltpu.VMEM((2, u_block, 2 * EMB), BF16),
            pltpu.VMEM((2, i_block, 2 * EMB), BF16),
            pltpu.VMEM((2, n_ia // 2, us, 2 * EMB), BF16),
            pltpu.VMEM((2, n_ia // 2, us, 2 * EMB), BF16),
            pltpu.VMEM((2, n_ia // 2, us, 2 * EMB), BF16),
            pltpu.VMEM((2, n_au, it, 2 * EMB), BF16),
            pltpu.VMEM((1, u_block), jnp.int32),
            pltpu.VMEM((n_au, 1, it), jnp.int32),
            pltpu.VMEM((1, slots), jnp.int32),
            pltpu.VMEM((1, slots), jnp.int32),
            pltpu.VMEM((1, slots), jnp.int32),
            pltpu.VMEM((1, 1), jnp.int32),
            pltpu.SemaphoreType.DMA((10,)),
            pltpu.SemaphoreType.DMA((4, n_ia)),
            pltpu.SemaphoreType.DMA((4, n_ia)),
            pltpu.SemaphoreType.DMA((4, n_au)),
            pltpu.SemaphoreType.DMA((4, n_au)),
        ],
        compiler_params=pltpu.CompilerParams(
            collective_id=0, has_side_effects=True, vmem_limit_bytes=48 * 1024 * 1024
        ),
    )(
        user_emb,
        item_emb,
        user_cot,
        item_cot,
        user_degree.reshape(1, -1),
        item_degree,
        tile_rows.reshape(1, -1),
        tile_cols.reshape(1, -1),
        tile_key.reshape(1, -1),
        tile_count,
    )


def solution(mesh):
    shards = P(("au", "ia"), None)
    in_specs = (
        shards,
        shards,
        shards,
        shards,
        P("au"),
        P(None, "ia", None),
        P("au", "ia", None),
        P("au", "ia", None),
        P("au", "ia", None),
        P("au", "ia"),
    )
    return jax.shard_map(
        functools.partial(per_device, mesh.shape["au"], mesh.shape["ia"]),
        mesh=mesh,
        in_specs=in_specs,
        out_specs=(shards,) * 4,
        check_vma=False,
    )
```
